32 devices in a mesh: groups: 2 (over y), domain: 4 (over z), band: 4 (over x, core).
Axes of the slice: x: 2, y: 2, z: 4, core: 2. Of those that a mesh axis runs over, the one named last changes fastest.
Arguments:
- orbitals: float32 [256, 32, 32, 128], P('band', 'domain', 'groups'), parts along dimension 2, may hold values from -48 to 48
- potential: float32 [32, 32, 128], P('domain', 'groups'), parts along dimension 1, may hold values from -1.5 to 0.5
- projector: float32 [48, 4, 256], P('domain', None, 'groups'), parts along dimension 2, may hold values from -0.5 to 0.5
- coupling: float32 [48, 8], P('domain', 'groups'), parts along dimension 1, may hold values from 1 to 4
- sphere_cells: int32 [48, 256], P('domain', 'groups'), parts along dimension 1, may hold values from 0 to 65535, as said below
- atom_count: int32 [8], P('groups'), parts along dimension 0, may hold values from 1 to 12, 32 in all
Outputs:
- filtered: float32 [256, 32, 32, 128], P('band', 'domain', 'groups'), parts along dimension 2
- gram: float32 [256, 512], P('band', 'groups'), parts along dimension 1
The draws below stay inside these ranges and needn't reach their ends.
There are 2 independent parts, one for each index of `groups`. The reference program is written for one: setup_inputs(seed, part) draws one part's arguments, and reference() takes and returns one part's arrays. A program takes and returns all parts, laid end to end along the dimension named above; each array names one. Nothing has to cross between parts.
Inputs may be any that keep to these rules, and one draw needn't show every extreme that they name: `sphere_cells`: each atom slot a holds 128 distinct cells chosen within the cube of side 2 * 5 + 1 (periodically) around a center cell whose first coordinate lies in [8 (a // 12), 8 (a // 12 + 1)); a cell's flat index is (x 16 + y) * 128 + z.
All inputs are finite; a program needn't handle non-finite values.
Results may differ from the reference program's by a relative error of at most 0.0001.
Values sent between devices are 32-bit elements; how exact they have to be, the bound alone decides.
A program may use at most 192 MiB of HBM per device.

```python
import math
import jax
import jax.numpy as jnp
import numpy as np
from jax import lax

NB = 256
CX = 8
NY = 16
NZ = 128
ATOM_DEV = 12
DEGREE = 2
RAD = 5
SPH = 128
NPROJ = 4
NX = 32
NATOM = 48
LIVE = 32
N_DOMAIN = 4


def draw_sphere_cells(key, part):
    key = jax.random.fold_in(key, 11)
    key_center, key_pick = jax.random.split(key)
    key_list = jax.random.split(key_center, 3)
    atom_total = ATOM_DEV * N_DOMAIN
    cube_side = 2 * RAD + 1
    cube_cells = cube_side * cube_side * cube_side
    owner_slab = jnp.arange(atom_total, dtype=jnp.int32) // ATOM_DEV
    center_x = owner_slab * CX + jax.random.randint(key_list[0], (atom_total,), 0, CX, dtype=jnp.int32)
    center_y = jax.random.randint(key_list[1], (atom_total,), 0, NY, dtype=jnp.int32)
    center_z = jax.random.randint(key_list[2], (atom_total,), 0, NZ, dtype=jnp.int32)
    scores = jax.random.randint(key_pick, (atom_total, cube_cells), 0, 2 ** 20, dtype=jnp.int32) * cube_cells + jnp.arange(cube_cells, dtype=jnp.int32)[None]
    chosen = jnp.argsort(scores, axis=1)[:, :SPH].astype(jnp.int32)
    offset_x = chosen // (cube_side * cube_side) - RAD
    offset_y = chosen // cube_side % cube_side - RAD
    offset_z = chosen % cube_side - RAD
    cell_x = (center_x[:, None] + offset_x) % NX
    cell_y = (center_y[:, None] + offset_y) % NY
    cell_z = (center_z[:, None] + offset_z) % NZ
    return ((cell_x * NY + cell_y) * NZ + cell_z).astype(jnp.int32)


def with_spikes(values, stream_key, source, target, shards_of, factor):
    def block_of(axis_at):
        return (jnp.arange(values.shape[axis_at]) // (values.shape[axis_at] // shards_of)).reshape((-1,) + (1,) * (values.ndim - 1 - axis_at))

    first = jax.random.permutation(stream_key, shards_of)[block_of(target)]
    other_side = (block_of(target) + shards_of // 2) % shards_of
    return jnp.where((block_of(source) == first) | (block_of(source) == other_side), factor * values, values)


def steps_of(own_key, dims, pieces, least, largest):
    def one(position, shards_of):
        steps = jax.random.uniform(jax.random.fold_in(jax.random.fold_in(own_key, 6), position), (shards_of,), jnp.float32, least / len(pieces), largest / len(pieces))
        return jnp.repeat(jnp.exp(steps), dims[position] // shards_of).reshape((-1,) + (1,) * (len(dims) - position - 1))

    level = one(*pieces[0])
    for cut in pieces[1:]:
        level = level * one(*cut)
    return level


def length_profile(number_of, total, reach, skew):
    weights = [(1 << 20) // math.isqrt(standing ** skew) + 1 for standing in range(2, number_of + 1)]
    surplus, counts = total - reach - (number_of - 1), [1] * (number_of - 1)
    while surplus > 0:
        movable = [i for i in range(number_of - 1) if counts[i] < reach]
        pool, left = sum([weights[i] for i in movable]), surplus
        for i in movable:
            more = min(reach - counts[i], max(1, left * weights[i] // pool), surplus)
            counts[i] = counts[i] + more
            surplus = surplus - more
    return np.array([reach] + counts)


def uneven(key, number_of, total, bound, lean):
    if number_of == 2:
        one = jax.random.randint(key, (), max(1, total - bound), min(bound, total - 1) + 1)
        return jnp.stack([one, total - one])
    tallies = jnp.asarray(length_profile(number_of, total, bound, lean), jnp.int32)
    twos = (number_of - 1) // 2
    donor, taker = tallies[1:1 + 2 * twos:2], tallies[2:2 + 2 * twos:2]
    room = jnp.minimum(donor - 1, bound - taker)
    moved = jax.random.randint(jax.random.fold_in(key, 1), (twos,), 0, 1 << 20) % (room + 1)
    tallies = tallies.at[1:1 + 2 * twos:2].set(donor - moved).at[2:2 + 2 * twos:2].set(taker + moved)
    return tallies[jax.random.permutation(jax.random.fold_in(key, 2), number_of)]


def gaussian(stream_key, dims, deviation, reach, cuts=(), kind=jnp.bfloat16):
    values = jax.random.normal(stream_key, dims, jnp.float32) * deviation
    if len(cuts) > 0:
        values = steps_of(stream_key, dims, cuts, -0.22, 0.18) * values
    return jnp.clip(values, min=-reach, max=reach).astype(kind)


def noise_with(rng, dims, scale, limit, cuts, heavy, held_as=jnp.bfloat16):
    array = scale * jax.random.normal(rng, dims, jnp.float32)
    if cuts:
        array = array * steps_of(rng, dims, cuts, -0.22, 0.18)
    return jnp.clip(with_spikes(array, jax.random.fold_in(rng, 3), *heavy), -limit, limit).astype(held_as)


def setup_inputs(seed: int = 0, part: int = 0) -> dict:
    key_of = jax.random.split(jax.random.key(seed), 7)
    part_keys = jax.random.split(jax.random.fold_in(key_of[6], part), 7)
    orbitals = noise_with(part_keys[0], (NB, NX, NY, NZ), 8.0, 48.0, ((0, 4), (1, 4)), (1, 0, 4, 2.0), jnp.float32)
    potential = jnp.clip(-1.5 + 2.0 * jax.random.uniform(part_keys[1], (NX, NY, NZ), jnp.float32) ** steps_of(part_keys[1], (NX, NY, NZ), ((0, 4),), -0.2, 0.2), -1.5, 0.5)
    projector = gaussian(part_keys[2], (NATOM, NPROJ, SPH), SPH ** -0.5, 0.5, ((0, 4),), jnp.float32)
    coupling = jnp.clip(jnp.exp(math.log(4.0) - 1.3862944 * jax.random.uniform(part_keys[3], (NATOM, NPROJ), jnp.float32) ** steps_of(part_keys[3], (NATOM, NPROJ), ((0, 4),), -0.2, 0.2)), 1.0, 4.0)
    sphere_cells = draw_sphere_cells(jax.random.fold_in(jax.random.fold_in(key_of[6], part), 71), part)
    atom_count = uneven(part_keys[5], N_DOMAIN, LIVE, ATOM_DEV, 2).astype(jnp.int32)
    return dict(orbitals=orbitals, potential=potential, projector=projector, coupling=coupling, sphere_cells=sphere_cells, atom_count=atom_count)


stencil_weights = (12.0 / 7.0, -15.0 / 56.0, 10.0 / 189.0, -1.0 / 112.0, 2.0 / 1925.0, -1.0 / 16632.0)
center_weight = -5369.0 / 1800.0
lower_edge = 2.0
upper_edge = 24.0
bottom_edge = -1.5


def filter_scales(degree_count):
    half_width = (upper_edge - lower_edge) / 2.0
    middle = (upper_edge + lower_edge) / 2.0
    ratio_first = half_width / (bottom_edge - middle)
    ratio_now = ratio_first
    scales = [(ratio_first / half_width, 0.0)]
    for number in range(degree_count - 1):
        ratio_next = 1.0 / (2.0 / ratio_first - ratio_now)
        scales.append((2.0 * ratio_next / half_width, ratio_now * ratio_next))
        ratio_now = ratio_next
    return middle, scales


def kinetic(orbital_block):
    summed = 3.0 * center_weight * orbital_block
    for offset, weight in enumerate(stencil_weights, start=1):
        for axis_dim in (1, 2, 3):
            summed = summed + weight * (jnp.roll(orbital_block, offset, axis_dim) + jnp.roll(orbital_block, -offset, axis_dim))
    return -0.5 * summed


def nonlocal_term(orbital_block, projector, strength, sphere_cells):
    band_count = orbital_block.shape[0]
    flattened = orbital_block.reshape(band_count, -1)
    picked = flattened[:, sphere_cells]
    projection = jnp.einsum("ajs,bas->baj", projector, picked, precision=lax.Precision.HIGHEST)
    weighted = projection * strength[None]
    images = jnp.einsum("ajs,baj->bas", projector, weighted, precision=lax.Precision.HIGHEST)
    result = jnp.zeros_like(flattened).at[:, sphere_cells].add(images)
    return result.reshape(orbital_block.shape)


def reference(orbitals, potential, projector, coupling, sphere_cells, atom_count):
    slots = jnp.arange(ATOM_DEV * N_DOMAIN).astype(jnp.int32)
    owners = (slots // ATOM_DEV).astype(jnp.int32)
    live = (slots % ATOM_DEV < atom_count[owners]).astype(jnp.float32)
    strength = coupling * live[:, None]
    middle, scales = filter_scales(DEGREE)

    def hamiltonian(orbital_block):
        return kinetic(orbital_block) + potential[None] * orbital_block + nonlocal_term(orbital_block, projector, strength, sphere_cells)

    def apply_filter(orbital_block):
        previous = orbital_block
        current = (hamiltonian(orbital_block) - middle * orbital_block) * scales[0][0]
        for scale_new, scale_old in scales[1:]:
            following = (hamiltonian(current) - middle * current) * scale_new - scale_old * previous
            previous, current = current, following
        return current

    grouped = orbitals.reshape(8, NB // 8, NX, NY, NZ)
    filtered = lax.map(apply_filter, grouped).reshape(NB, NX, NY, NZ)
    flattened = filtered.reshape(NB, -1)
    gram = jnp.dot(flattened, flattened.T, precision=lax.Precision.HIGHEST, preferred_element_type=jnp.float32) / (NX * NY * NZ)
    return filtered, gram
```

```python
import functools

import jax
import jax.numpy as jnp
from jax import lax
from jax.experimental import pallas as pl
from jax.experimental.pallas import tpu as pltpu
from jax.sharding import PartitionSpec as P

stencil_weights = (
    12.0 / 7.0,
    -15.0 / 56.0,
    10.0 / 189.0,
    -1.0 / 112.0,
    2.0 / 1925.0,
    -1.0 / 16632.0,
)
center_weight = -5369.0 / 1800.0
HALO = len(stencil_weights)
REACH = 5
MIDDLE = 13.0
HALF_WIDTH = 11.0
RATIO_1 = HALF_WIDTH / (-1.5 - MIDDLE)
RATIO_2 = 1.0 / (2.0 / RATIO_1 - RATIO_1)
SCALE_1 = RATIO_1 / HALF_WIDTH
SCALE_2 = 2.0 * RATIO_2 / HALF_WIDTH
SCALE_OLD = RATIO_1 * RATIO_2
VMEM = 56 * 1024 * 1024

NT = (((1,), (1,)), ((), ()))
NN = (((1,), (0,)), ((), ()))


def split(values):
    high = values.astype(jnp.bfloat16)
    low = (values - high.astype(jnp.float32)).astype(jnp.bfloat16)
    return high, low


def dot(a, b, dims):
    return lax.dot_general(a, b, dims, preferred_element_type=jnp.float32)


def dot3(a, b, dims):
    return dot(a[0], b[0], dims) + (dot(a[0], b[1], dims) + dot(a[1], b[0], dims))


def kinetic_weight(distance):
    table = jnp.where(distance == 0, -0.5 * center_weight, 0.0)
    for offset, weight in enumerate(stencil_weights, start=1):
        table = jnp.where(distance == offset, -0.5 * weight, table)
    return table


def periodic(difference, count):
    difference = jnp.abs(difference)
    return jnp.minimum(difference, count - difference)


def build_kernel(nx, ny, slab, x_ref, y_ref, z_ref, proj_ref, pot_ref, out_ref):
    rows = slab * ny
    nz = pot_ref.shape[-1]
    sph = proj_ref.shape[-1]
    row = lax.broadcasted_iota(jnp.int32, (rows, sph), 0)
    dx = periodic(row // ny - x_ref[0], nx)
    dy = periodic(row % ny - y_ref[0], ny)
    dz = periodic(lax.broadcasted_iota(jnp.int32, (nz, sph), 0) - z_ref[0], nz)
    same_x, same_y = dx == 0, dy == 0
    here = jnp.where(same_x & same_y, 1.0, 0.0)
    near = jnp.where(same_y, kinetic_weight(dx), 0.0) + jnp.where(same_x, kinetic_weight(dy), 0.0)
    point = jnp.where(dz == 0, 1.0, 0.0).astype(jnp.bfloat16)
    along_high, along_low = split(kinetic_weight(dz))
    none = jnp.zeros_like(point)
    right = jnp.concatenate(
        [jnp.concatenate([point, along_high], 1), jnp.concatenate([none, point], 1)], 0
    )
    fine = jnp.concatenate([none, along_low], 1)
    for j in range(proj_ref.shape[1]):
        values = proj_ref[0, j : j + 1, :]
        left = jnp.concatenate([near * values, here * values], 1)
        high, low = split(left)
        both = dot(high, right, NT) + dot(low, right, NT)
        plain = both[:, nz:]
        acted = both[:, :nz] + dot(high, fine, NT) + pot_ref[...] * plain
        flat = out_ref.reshape(rows * out_ref.shape[1], nz)
        nj = proj_ref.shape[1]
        flat[pl.ds(j, rows, stride=2 * nj), :] = acted
        flat[pl.ds(nj + j, rows, stride=2 * nj), :] = plain


def project_kernel(chunk, pq_ref, v_ref, out_ref, over_ref):
    @pl.when(pl.program_id(0) == 0)
    def _():
        out_ref[...] = jnp.zeros_like(out_ref)
        over_ref[...] = jnp.zeros_like(over_ref)

    bands, _, nz = v_ref.shape
    flat = v_ref.reshape(bands * chunk, nz)
    for r in range(0, chunk, 2):
        pq = jnp.concatenate([pq_ref[r], pq_ref[r + 1]], 1)
        v = jnp.concatenate(
            [flat[pl.ds(r, bands, stride=chunk), :], flat[pl.ds(r + 1, bands, stride=chunk), :]], 1
        )
        pq, v = split(pq), split(v)
        out_ref[...] += dot3(pq, v, NT)
        over_ref[...] += dot3(pq, pq, NT)


def local_kernel(v_ref, pot_ref, table_ref, out_ref, pad_ref, mid_ref):
    parts, _, slab, ny, nz = v_ref.shape
    nx = parts * slab
    step = 4
    table_high, table_low = split(table_ref[...])
    both_rows = jnp.concatenate([table_high, table_high], 0)

    def fill(read):
        for p in range(parts):
            pad_ref[pl.ds(HALO + p * slab, slab)] = read(p)
        pad_ref[pl.ds(0, HALO)] = pad_ref[pl.ds(nx, HALO)]
        pad_ref[pl.ds(HALO + nx, HALO)] = pad_ref[pl.ds(HALO, HALO)]

    def apply(start):
        center = pad_ref[pl.ds(HALO + start, step)]
        total = (-center_weight) * center
        for k, weight in enumerate(stencil_weights, start=1):
            around = (
                pad_ref[pl.ds(HALO + start + k, step)]
                + pad_ref[pl.ds(HALO + start - k, step)]
                + pltpu.roll(center, k, 1)
                + pltpu.roll(center, ny - k, 1)
            )
            total = total + (-0.5 * weight) * around
        high, low = split(center.reshape(step * ny, nz))
        along = dot(jnp.concatenate([high, low], 1), both_rows, NN) + dot(high, table_low, NN)
        total = total + along.reshape(step, ny, nz)
        return center, total + (pot_ref[pl.ds(start, step)] - MIDDLE) * center

    fill(lambda p: v_ref[p, 0])

    @pl.loop(0, nx // step)
    def _(i):
        _, acted = apply(i * step)
        mid_ref[pl.ds(i * step, step)] = SCALE_1 * acted

    fill(lambda p: mid_ref[pl.ds(p * slab, slab)])

    @pl.loop(0, nx // step)
    def _(i):
        _, acted = apply(i * step)
        each = slab // step
        p, q = i // each, i % each
        old = v_ref[p, 0, pl.ds(q * step, step)]
        out_ref[p, 0, pl.ds(q * step, step)] = SCALE_2 * acted - SCALE_OLD * old


def expand_kernel(chunk, pq_ref, coef_ref, y_ref, f_ref, g_ref):
    bands, _, nz = y_ref.shape
    coef = split(coef_ref[...])
    flat_y = y_ref.reshape(bands * chunk, nz)
    flat_f = f_ref.reshape(bands * chunk, nz)
    for r in range(chunk):
        total = dot3(coef, split(pq_ref[r]), NN) + flat_y[pl.ds(r, bands, stride=chunk), :]
        flat_f[pl.ds(r, bands, stride=chunk), :] = total
        g_ref[r] = total


def gram_kernel(chunk, x_ref, out_ref):
    @pl.when(pl.program_id(0) == 0)
    def _():
        out_ref[...] = jnp.zeros_like(out_ref)

    count, _, bands, nz = x_ref.shape
    for r in range(0, chunk, 2):
        x = jnp.concatenate(
            [x_ref[:, r].reshape(count * bands, nz), x_ref[:, r + 1].reshape(count * bands, nz)], 1
        )
        x = split(x)
        out_ref[...] += dot3(x, x, NT)


def call(kernel, **options):
    return pl.pallas_call(
        kernel, compiler_params=pltpu.CompilerParams(vmem_limit_bytes=VMEM), **options
    )


def per_device(orbitals, potential, projector, coupling, sphere_cells, atom_count):
    f32 = jnp.float32
    bands, slab, ny, nz = orbitals.shape
    slots, nj, sph = projector.shape
    nd, nb = lax.axis_size("domain"), lax.axis_size("band")
    nx, plane, rows = slab * nd, ny * nz, slab * ny
    pos = lax.axis_index("domain")
    share = bands // nd

    spread = lax.all_to_all(orbitals.reshape(nd, share, slab, ny, nz), "domain", 0, 0)
    pot_all = lax.all_gather(potential, "domain", axis=0, tiled=True)
    index = jnp.arange(nz, dtype=jnp.int32)
    table = kinetic_weight(periodic(index[:, None] - index[None, :], nz)).astype(f32)
    block = pl.BlockSpec((nd, 1, slab, ny, nz), lambda b: (0, b, 0, 0, 0))
    local = call(
        local_kernel,
        grid=(share,),
        in_specs=[
            block,
            pl.BlockSpec((nx, ny, nz), lambda b: (0, 0, 0)),
            pl.BlockSpec((nz, nz), lambda b: (0, 0)),
        ],
        out_specs=block,
        out_shape=jax.ShapeDtypeStruct(spread.shape, f32),
        scratch_shapes=[pltpu.VMEM((nx + 2 * HALO, ny, nz), f32), pltpu.VMEM((nx, ny, nz), f32)],
    )(spread, pot_all, table)
    local = lax.all_to_all(local, "domain", 0, 0).reshape(bands, rows, nz)

    near = -(-(REACH + HALO) // slab)
    proj_all = lax.all_gather(projector, "domain", axis=0, tiled=False)
    cells_all = lax.all_gather(sphere_cells, "domain", axis=0, tiled=False)
    coupling_all = lax.all_gather(coupling, "domain", axis=0, tiled=True)
    if nd <= 2 * near + 1:
        sources = jnp.arange(nd, dtype=jnp.int32)
    else:
        sources = (pos + jnp.arange(-near, near + 1, dtype=jnp.int32)) % nd
    atoms = sources.shape[0] * slots
    proj_near = proj_all[sources].reshape(atoms, nj, sph)
    cells = cells_all[sources].reshape(atoms, 1, sph)
    cell_x = (cells // plane - pos * slab) % nx
    per_atom = pl.BlockSpec((1, 1, sph), lambda a: (a, 0, 0))
    count = atoms * 2 * nj
    pq = call(
        functools.partial(build_kernel, nx, ny, slab),
        grid=(atoms,),
        in_specs=[
            per_atom,
            per_atom,
            per_atom,
            pl.BlockSpec((1, nj, sph), lambda a: (a, 0, 0)),
            pl.BlockSpec((rows, nz), lambda a: (0, 0)),
        ],
        out_specs=pl.BlockSpec((rows, 2 * nj, nz), lambda a: (0, a, 0)),
        out_shape=jax.ShapeDtypeStruct((rows, count, nz), f32),
    )(cell_x, cells // nz % ny, cells % nz, proj_near, potential.reshape(rows, nz))

    chunk = 8
    part_out, part_over = call(
        functools.partial(project_kernel, chunk),
        grid=(rows // chunk,),
        in_specs=[
            pl.BlockSpec((chunk, count, nz), lambda i: (i, 0, 0)),
            pl.BlockSpec((bands, chunk, nz), lambda i: (0, i, 0)),
        ],
        out_specs=[
            pl.BlockSpec((count, bands), lambda i: (0, 0)),
            pl.BlockSpec((count, count), lambda i: (0, 0)),
        ],
        out_shape=[
            jax.ShapeDtypeStruct((count, bands), f32),
            jax.ShapeDtypeStruct((count, count), f32),
        ],
    )(pq, orbitals.reshape(bands, rows, nz))
    width = atoms * nj
    part_out = part_out.reshape(atoms, 2, nj, bands)
    part_over = part_over.reshape(atoms, 2, nj, atoms, 2, nj)[:, 1, :, :, 1, :].reshape(width, width)
    parts = jnp.concatenate(
        [
            part_out[:, 0].reshape(width, bands),
            part_out[:, 1].reshape(width, bands),
        ],
        1,
    )
    total = nd * slots * nj
    if total != width:
        where = (sources[:, None] * (slots * nj) + jnp.arange(slots * nj)[None]).reshape(-1)
        parts = jnp.zeros((total, 2 * bands), f32).at[where].set(parts)
        part_over = jnp.zeros((total, total), f32).at[where[:, None], where[None, :]].set(part_over)
    summed = lax.psum(jnp.concatenate([parts, part_over], 1), "domain")
    acted, plain, over = (
        summed[:, :bands],
        summed[:, bands : 2 * bands],
        summed[:, 2 * bands :],
    )
    slot = jnp.arange(slots, dtype=jnp.int32)
    live = (slot[None, :] < atom_count[:, None]).reshape(-1)
    strength = jnp.where(live[:, None], coupling_all, 0.0).reshape(-1, 1)
    weight_0 = strength * plain
    plain_1 = SCALE_1 * (
        acted + jnp.dot(over, weight_0, precision=lax.Precision.HIGHEST) - MIDDLE * plain
    )
    coef_p = SCALE_2 * (strength * plain_1 - (MIDDLE * SCALE_1) * weight_0)
    coef_q = (SCALE_2 * SCALE_1) * weight_0
    coef = jnp.stack(
        [coef_q.reshape(nd, slots, nj, bands), coef_p.reshape(nd, slots, nj, bands)], 2
    )
    coef = coef[sources].reshape(count, bands).T

    filtered, shared = call(
        functools.partial(expand_kernel, chunk),
        grid=(rows // chunk,),
        in_specs=[
            pl.BlockSpec((chunk, count, nz), lambda i: (i, 0, 0)),
            pl.BlockSpec((bands, count), lambda i: (0, 0)),
            pl.BlockSpec((bands, chunk, nz), lambda i: (0, i, 0)),
        ],
        out_specs=[
            pl.BlockSpec((bands, chunk, nz), lambda i: (0, i, 0)),
            pl.BlockSpec((chunk, bands, nz), lambda i: (i, 0, 0)),
        ],
        out_shape=[
            jax.ShapeDtypeStruct((bands, rows, nz), f32),
            jax.ShapeDtypeStruct((rows, bands, nz), f32),
        ],
    )(pq, coef, local)

    shared = lax.all_to_all(shared.reshape(nb, rows // nb, bands, nz), "band", 0, 0)
    gram = call(
        functools.partial(gram_kernel, chunk),
        grid=(rows // nb // chunk,),
        in_specs=[pl.BlockSpec((nb, chunk, bands, nz), lambda i: (0, i, 0, 0))],
        out_specs=pl.BlockSpec((nb * bands, nb * bands), lambda i: (0, 0)),
        out_shape=jax.ShapeDtypeStruct((nb * bands, nb * bands), f32),
    )(shared)
    gram = lax.psum(gram, ("domain", "band"))
    gram = lax.dynamic_slice_in_dim(gram, lax.axis_index("band") * bands, bands, 0)
    return filtered.reshape(orbitals.shape), gram / (nx * plane)


def solution(mesh):
    placed = (
        P("band", "domain", "groups", None),
        P("domain", "groups", None),
        P("domain", None, "groups"),
        P("domain", "groups"),
        P("domain", "groups"),
        P("groups"),
    )
    return jax.shard_map(
        per_device,
        mesh=mesh,
        in_specs=placed,
        out_specs=(P("band", "domain", "groups", None), P("band", "groups")),
        check_vma=False,
    )
```

```python
import functools

import jax
import jax.numpy as jnp
from jax import lax
from jax.experimental import pallas as pl
from jax.experimental.pallas import tpu as pltpu
from jax.sharding import PartitionSpec as P

stencil_weights = (
    12.0 / 7.0,
    -15.0 / 56.0,
    10.0 / 189.0,
    -1.0 / 112.0,
    2.0 / 1925.0,
    -1.0 / 16632.0,
)
center_weight = -5369.0 / 1800.0
HALO = len(stencil_weights)
REACH = 5
MIDDLE = 13.0
HALF_WIDTH = 11.0
RATIO_1 = HALF_WIDTH / (-1.5 - MIDDLE)
RATIO_2 = 1.0 / (2.0 / RATIO_1 - RATIO_1)
SCALE_1 = RATIO_1 / HALF_WIDTH
SCALE_2 = 2.0 * RATIO_2 / HALF_WIDTH
SCALE_OLD = RATIO_1 * RATIO_2
VMEM = 56 * 1024 * 1024

NT = (((1,), (1,)), ((), ()))
NN = (((1,), (0,)), ((), ()))


def split(values):
    high = values.astype(jnp.bfloat16)
    low = (values - high.astype(jnp.float32)).astype(jnp.bfloat16)
    return high, low


def dot(a, b, dims):
    return lax.dot_general(a, b, dims, preferred_element_type=jnp.float32)


def dot3(a, b, dims):
    return dot(a[0], b[0], dims) + (dot(a[0], b[1], dims) + dot(a[1], b[0], dims))


def kinetic_weight(distance):
    table = jnp.where(distance == 0, -0.5 * center_weight, 0.0)
    for offset, weight in enumerate(stencil_weights, start=1):
        table = jnp.where(distance == offset, -0.5 * weight, table)
    return table


def periodic(difference, count):
    difference = jnp.abs(difference)
    return jnp.minimum(difference, count - difference)


def build_kernel(nx, ny, slab, x_ref, y_ref, z_ref, proj_ref, pot_ref, out_ref):
    rows = slab * ny
    nz = pot_ref.shape[-1]
    sph = proj_ref.shape[-1]
    row = lax.broadcasted_iota(jnp.int32, (rows, sph), 0)
    dx = periodic(row // ny - x_ref[0], nx)
    dy = periodic(row % ny - y_ref[0], ny)
    dz = periodic(lax.broadcasted_iota(jnp.int32, (nz, sph), 0) - z_ref[0], nz)
    same_x, same_y = dx == 0, dy == 0
    here = jnp.where(same_x & same_y, 1.0, 0.0)
    near = jnp.where(same_y, kinetic_weight(dx), 0.0) + jnp.where(same_x, kinetic_weight(dy), 0.0)
    point = jnp.where(dz == 0, 1.0, 0.0).astype(jnp.bfloat16)
    along_high, along_low = split(kinetic_weight(dz))
    none = jnp.zeros_like(point)
    right = jnp.concatenate(
        [jnp.concatenate([point, along_high], 1), jnp.concatenate([none, point], 1)], 0
    )
    fine = jnp.concatenate([none, along_low], 1)
    for j in range(proj_ref.shape[1]):
        values = proj_ref[0, j : j + 1, :]
        left = jnp.concatenate([near * values, here * values], 1)
        high, low = split(left)
        both = dot(high, right, NT) + dot(low, right, NT)
        plain = both[:, nz:]
        acted = both[:, :nz] + dot(high, fine, NT) + pot_ref[...] * plain
        flat = out_ref.reshape(rows * out_ref.shape[1], nz)
        nj = proj_ref.shape[1]
        flat[pl.ds(j, rows, stride=2 * nj), :] = acted
        flat[pl.ds(nj + j, rows, stride=2 * nj), :] = plain


def project_kernel(chunk, pq_ref, v_ref, out_ref, over_ref):
    @pl.when(pl.program_id(0) == 0)
    def _():
        out_ref[...] = jnp.zeros_like(out_ref)
        over_ref[...] = jnp.zeros_like(over_ref)

    bands, _, nz = v_ref.shape
    flat = v_ref.reshape(bands * chunk, nz)
    for r in range(0, chunk, 2):
        pq = jnp.concatenate([pq_ref[r], pq_ref[r + 1]], 1)
        v = jnp.concatenate(
            [flat[pl.ds(r, bands, stride=chunk), :], flat[pl.ds(r + 1, bands, stride=chunk), :]], 1
        )
        pq, v = split(pq), split(v)
        out_ref[...] += dot3(pq, v, NT)
        over_ref[...] += dot3(pq, pq, NT)


def local_kernel(parts, *refs):
    v_refs, (pot_ref, table_ref) = refs[:parts], refs[parts : parts + 2]
    out_refs, (pad_ref, mid_ref) = refs[parts + 2 : 2 * parts + 2], refs[2 * parts + 2 :]
    _, slab, ny, nz = v_refs[0].shape
    nx = parts * slab
    step = 4
    table_high, table_low = split(table_ref[...])
    both_rows = jnp.concatenate([table_high, table_high], 0)

    def fill(read):
        for p in range(parts):
            pad_ref[pl.ds(HALO + p * slab, slab)] = read(p)
        pad_ref[pl.ds(0, HALO)] = pad_ref[pl.ds(nx, HALO)]
        pad_ref[pl.ds(HALO + nx, HALO)] = pad_ref[pl.ds(HALO, HALO)]

    def apply(start):
        center = pad_ref[pl.ds(HALO + start, step)]
        total = (-center_weight) * center
        for k, weight in enumerate(stencil_weights, start=1):
            around = (
                pad_ref[pl.ds(HALO + start + k, step)]
                + pad_ref[pl.ds(HALO + start - k, step)]
                + pltpu.roll(center, k, 1)
                + pltpu.roll(center, ny - k, 1)
            )
            total = total + (-0.5 * weight) * around
        high, low = split(center.reshape(step * ny, nz))
        along = dot(jnp.concatenate([high, low], 1), both_rows, NN) + dot(high, table_low, NN)
        total = total + along.reshape(step, ny, nz)
        return total + (pot_ref[pl.ds(start, step)] - MIDDLE) * center

    fill(lambda p: v_refs[p][0])

    @pl.loop(0, nx // step)
    def _(i):
        mid_ref[pl.ds(i * step, step)] = SCALE_1 * apply(i * step)

    fill(lambda p: mid_ref[pl.ds(p * slab, slab)])

    for p in range(parts):

        @pl.loop(0, slab // step)
        def _(i, p=p):
            old = v_refs[p][0, pl.ds(i * step, step)]
            acted = apply(p * slab + i * step)
            out_refs[p][0, pl.ds(i * step, step)] = SCALE_2 * acted - SCALE_OLD * old


def expand_kernel(chunk, parts, halves, pos_ref, pq_ref, coef_ref, *refs):
    y_refs, (f_ref, g_ref) = refs[: parts * halves], refs[parts * halves :]
    each, _, nz = y_refs[0].shape
    bands = f_ref.shape[0]
    flat_y = [y_ref.reshape(each * chunk, nz) for y_ref in y_refs]
    flat_f = f_ref.reshape(bands * chunk, nz)
    coef = split(coef_ref[...])
    for r in range(chunk):
        added = dot3(coef, split(pq_ref[r]), NN)
        for p in range(parts):
            for h in range(halves):
                first = (p * halves + h) * each
                total = (
                    added[first : first + each]
                    + flat_y[p * halves + h][pl.ds(r, each, stride=chunk), :]
                )
                to = lax.rem(pos_ref[0] + p, parts) * (halves * each) + h * each
                flat_f[pl.ds(to * chunk + r, each, stride=chunk), :] = total
                g_ref[r, pl.ds(pl.multiple_of(to, each), each), :] = total


def gram_kernel(chunk, count, pos_ref, *refs):
    x_refs, (out_ref, x_scratch) = refs[:count], refs[count:]

    @pl.when(pl.program_id(0) == 0)
    def _():
        out_ref[...] = jnp.zeros_like(out_ref)

    _, bands, nz = x_refs[0].shape
    for r in range(0, chunk, 2):
        for p in range(count):
            at = pl.multiple_of(lax.rem(pos_ref[0] + count - p, count) * bands, bands)
            x_scratch[pl.ds(at, bands), :] = jnp.concatenate([x_refs[p][r], x_refs[p][r + 1]], 1)
        x = split(x_scratch[...])
        out_ref[...] += dot3(x, x, NT)


def shifted(values, axis, by):
    count = lax.axis_size(axis)
    return lax.ppermute(values, axis, [(i, (i + by) % count) for i in range(count)])


def summed_over(values, axis):
    count = lax.axis_size(axis)
    if count > 8:
        return lax.psum(values, axis)
    total = values
    for p in range(1, count):
        total = total + shifted(values, axis, p)
    return total


def block_of(values, index, count):
    size = values.shape[0] // count
    return lax.dynamic_slice_in_dim(values, index % count * size, size, 0)


def cost(flops, moved):
    return pl.CostEstimate(flops=flops, bytes_accessed=moved, transcendentals=0)


def call(kernel, **options):
    return pl.pallas_call(
        kernel, compiler_params=pltpu.CompilerParams(vmem_limit_bytes=VMEM), **options
    )


def per_device(orbitals, potential, projector, coupling, sphere_cells, atom_count):
    f32 = jnp.float32
    bands, slab, ny, nz = orbitals.shape
    slots, nj, sph = projector.shape
    nd, nb = lax.axis_size("domain"), lax.axis_size("band")
    nx, plane, rows = slab * nd, ny * nz, slab * ny
    pos = lax.axis_index("domain")
    share = bands // nd
    halves = 2 if share % 2 == 0 else 1
    each = share // halves

    pot_all = lax.all_gather(potential, "domain", axis=0, tiled=True)
    pot_all = lax.dynamic_slice_in_dim(
        jnp.concatenate([pot_all, pot_all], 0), pos * slab, nx, 0
    )
    index = jnp.arange(nz, dtype=jnp.int32)
    table = kinetic_weight(periodic(index[:, None] - index[None, :], nz)).astype(f32)
    block = pl.BlockSpec((1, slab, ny, nz), lambda b: (b, 0, 0, 0))

    def sent(h, p):
        start = (pos - p) % nd * share + h * each
        part = lax.dynamic_slice_in_dim(orbitals, start, each, 0)
        return shifted(part, "domain", -p) if p else part

    local = []
    for h in range(halves):
        spread = [sent(h, p) for p in range(nd)]
        results = call(
            functools.partial(local_kernel, nd),
            grid=(each,),
            in_specs=[block] * nd
            + [
                pl.BlockSpec((nx, ny, nz), lambda b: (0, 0, 0)),
                pl.BlockSpec((nz, nz), lambda b: (0, 0)),
            ],
            out_specs=[block] * nd,
            out_shape=[jax.ShapeDtypeStruct(spread[0].shape, f32)] * nd,
            scratch_shapes=[
                pltpu.VMEM((nx + 2 * HALO, ny, nz), f32),
                pltpu.VMEM((nx, ny, nz), f32),
            ],
            cost_estimate=cost(share * nx * plane * 6000, share * nx * plane * 4),
        )(*spread, pot_all, table)
        local.append([shifted(part, "domain", p) if p else part for p, part in enumerate(results)])

    near = -(-(REACH + HALO) // slab)
    proj_all = lax.all_gather(projector, "domain", axis=0, tiled=False)
    cells_all = lax.all_gather(sphere_cells, "domain", axis=0, tiled=False)
    coupling_all = lax.all_gather(coupling, "domain", axis=0, tiled=True)
    if nd <= 2 * near + 1:
        sources = jnp.arange(nd, dtype=jnp.int32)
    else:
        sources = (pos + jnp.arange(-near, near + 1, dtype=jnp.int32)) % nd
    atoms = sources.shape[0] * slots
    proj_near = proj_all[sources].reshape(atoms, nj, sph)
    cells = cells_all[sources].reshape(atoms, 1, sph)
    cell_x = (cells // plane - pos * slab) % nx
    per_atom = pl.BlockSpec((1, 1, sph), lambda a: (a, 0, 0))
    count = atoms * 2 * nj
    pq = call(
        functools.partial(build_kernel, nx, ny, slab),
        grid=(atoms,),
        in_specs=[
            per_atom,
            per_atom,
            per_atom,
            pl.BlockSpec((1, nj, sph), lambda a: (a, 0, 0)),
            pl.BlockSpec((rows, nz), lambda a: (0, 0)),
        ],
        out_specs=pl.BlockSpec((rows, 2 * nj, nz), lambda a: (0, a, 0)),
        out_shape=jax.ShapeDtypeStruct((rows, count, nz), f32),
        cost_estimate=cost(atoms * 600_000_000, rows * count * nz * 4),
    )(cell_x, cells // nz % ny, cells % nz, proj_near, potential.reshape(rows, nz))

    chunk = 8
    part_out, part_over = call(
        functools.partial(project_kernel, chunk),
        grid=(rows // chunk,),
        in_specs=[
            pl.BlockSpec((chunk, count, nz), lambda i: (i, 0, 0)),
            pl.BlockSpec((bands, chunk, nz), lambda i: (0, i, 0)),
        ],
        out_specs=[
            pl.BlockSpec((count, bands), lambda i: (0, 0)),
            pl.BlockSpec((count, count), lambda i: (0, 0)),
        ],
        out_shape=[
            jax.ShapeDtypeStruct((count, bands), f32),
            jax.ShapeDtypeStruct((count, count), f32),
        ],
        cost_estimate=cost(rows * nz * count * (count + bands) * 8, rows * count * nz * 4),
    )(pq, orbitals.reshape(bands, rows, nz))
    slot = jnp.arange(slots, dtype=jnp.int32)
    live = (slot[None, :] < atom_count[:, None]).reshape(-1)
    strength = jnp.where(live[:, None], coupling_all, 0.0)
    highest = lax.Precision.HIGHEST
    if count == nd * slots * 2 * nj:
        summed = lax.psum(jnp.concatenate([part_out, part_over], 1), "domain")
        both, over = summed[:, :bands], summed[:, bands:]
        strength = jnp.concatenate([jnp.zeros_like(strength), strength], 1).reshape(-1, 1)
        weight_0 = strength * both
        plain_1 = SCALE_1 * (
            jnp.roll(both, nj, 0) + jnp.dot(over, weight_0, precision=highest) - MIDDLE * both
        )
        coef = SCALE_2 * (
            strength * plain_1
            - (MIDDLE * SCALE_1) * weight_0
            + SCALE_1 * jnp.roll(weight_0, -nj, 0)
        )
    else:
        width, total = atoms * nj, nd * slots * nj
        out = part_out.reshape(atoms, 2, nj, bands)
        over = part_over.reshape(atoms, 2, nj, atoms, 2, nj)[:, 1, :, :, 1, :].reshape(width, width)
        both = jnp.concatenate([out[:, 0].reshape(width, bands), out[:, 1].reshape(width, bands)], 1)
        where = (sources[:, None] * (slots * nj) + jnp.arange(slots * nj)[None]).reshape(-1)
        both = jnp.zeros((total, 2 * bands), f32).at[where].set(both)
        over = jnp.zeros((total, total), f32).at[where[:, None], where[None, :]].set(over)
        both, over = lax.psum(both, "domain"), lax.psum(over, "domain")
        acted, plain = both[:, :bands], both[:, bands:]
        strength = strength.reshape(-1, 1)
        weight_0 = strength * plain
        plain_1 = SCALE_1 * (
            acted + jnp.dot(over, weight_0, precision=highest) - MIDDLE * plain
        )
        coef_p = SCALE_2 * (strength * plain_1 - (MIDDLE * SCALE_1) * weight_0)
        coef_q = (SCALE_2 * SCALE_1) * weight_0
        coef = jnp.stack(
            [coef_q.reshape(nd, slots, nj, bands), coef_p.reshape(nd, slots, nj, bands)], 2
        )
        coef = coef[sources].reshape(count, bands)
    coef = jnp.concatenate([coef, coef], 1).T
    coef = lax.dynamic_slice_in_dim(coef, pos * share, bands, 0)

    smem = pl.BlockSpec(memory_space=pltpu.SMEM)
    part_block = pl.BlockSpec((each, chunk, nz), lambda i: (0, i, 0))
    came = [local[h][(nd - p) % nd].reshape(each, rows, nz) for p in range(nd) for h in range(halves)]
    filtered, shared = call(
        functools.partial(expand_kernel, chunk, nd, halves),
        grid=(rows // chunk,),
        in_specs=[
            smem,
            pl.BlockSpec((chunk, count, nz), lambda i: (i, 0, 0)),
            pl.BlockSpec((bands, count), lambda i: (0, 0)),
        ]
        + [part_block] * (nd * halves),
        out_specs=[
            pl.BlockSpec((bands, chunk, nz), lambda i: (0, i, 0)),
            pl.BlockSpec((chunk, bands, nz), lambda i: (i, 0, 0)),
        ],
        out_shape=[
            jax.ShapeDtypeStruct((bands, rows, nz), f32),
            jax.ShapeDtypeStruct((rows, bands, nz), f32),
        ],
    )(pos.reshape(1), pq, coef, *came)

    band = lax.axis_index("band")
    given = [block_of(shared, band + p, nb) for p in range(nb)]
    given = [shifted(part, "band", p) if p else part for p, part in enumerate(given)]
    gram = call(
        functools.partial(gram_kernel, chunk, nb),
        grid=(rows // nb // chunk,),
        in_specs=[smem] + [pl.BlockSpec((chunk, bands, nz), lambda i: (i, 0, 0))] * nb,
        out_specs=pl.BlockSpec((nb * bands, nb * bands), lambda i: (0, 0)),
        out_shape=jax.ShapeDtypeStruct((nb * bands, nb * bands), f32),
        scratch_shapes=[pltpu.VMEM((nb * bands, 2 * nz), f32)],
    )(band.reshape(1), *given)
    own = block_of(gram, band, nb)
    for p in range(1, nb):
        own = own + shifted(block_of(gram, band + p, nb), "band", p)
    own = summed_over(own, "domain")
    return filtered.reshape(orbitals.shape), own / (nx * plane)


def solution(mesh):
    placed = (
        P("band", "domain", "groups", None),
        P("domain", "groups", None),
        P("domain", None, "groups"),
        P("domain", "groups"),
        P("domain", "groups"),
        P("groups"),
    )
    return jax.shard_map(
        per_device,
        mesh=mesh,
        in_specs=placed,
        out_specs=(P("band", "domain", "groups", None), P("band", "groups")),
        check_vma=False,
    )
```

```python
import functools

import jax
import jax.numpy as jnp
from jax import lax
from jax.experimental import pallas as pl
from jax.experimental.pallas import tpu as pltpu
from jax.sharding import PartitionSpec as P

stencil_weights = (
    12.0 / 7.0,
    -15.0 / 56.0,
    10.0 / 189.0,
    -1.0 / 112.0,
    2.0 / 1925.0,
    -1.0 / 16632.0,
)
center_weight = -5369.0 / 1800.0
HALO = len(stencil_weights)
REACH = 5
MIDDLE = 13.0
HALF_WIDTH = 11.0
RATIO_1 = HALF_WIDTH / (-1.5 - MIDDLE)
RATIO_2 = 1.0 / (2.0 / RATIO_1 - RATIO_1)
SCALE_1 = RATIO_1 / HALF_WIDTH
SCALE_2 = 2.0 * RATIO_2 / HALF_WIDTH
SCALE_OLD = RATIO_1 * RATIO_2
VMEM = 56 * 1024 * 1024

NT = (((1,), (1,)), ((), ()))
NN = (((1,), (0,)), ((), ()))


def split(values):
    high = values.astype(jnp.bfloat16)
    low = (values - high.astype(jnp.float32)).astype(jnp.bfloat16)
    return high, low


def dot(a, b, dims):
    return lax.dot_general(a, b, dims, preferred_element_type=jnp.float32)


def dot3(a, b, dims):
    return dot(a[0], b[0], dims) + (dot(a[0], b[1], dims) + dot(a[1], b[0], dims))


def kinetic_weight(distance):
    table = jnp.where(distance == 0, -0.5 * center_weight, 0.0)
    for offset, weight in enumerate(stencil_weights, start=1):
        table = jnp.where(distance == offset, -0.5 * weight, table)
    return table


def periodic(difference, count):
    difference = jnp.abs(difference)
    return jnp.minimum(difference, count - difference)


def build_kernel(nx, ny, slab, x_ref, y_ref, z_ref, proj_ref, pot_ref, out_ref):
    rows = slab * ny
    nz = pot_ref.shape[-1]
    sph = proj_ref.shape[-1]
    row = lax.broadcasted_iota(jnp.int32, (rows, sph), 0)
    dx = periodic(row // ny - x_ref[0], nx)
    dy = periodic(row % ny - y_ref[0], ny)
    dz = periodic(lax.broadcasted_iota(jnp.int32, (nz, sph), 0) - z_ref[0], nz)
    same_x, same_y = dx == 0, dy == 0
    here = jnp.where(same_x & same_y, 1.0, 0.0)
    near = jnp.where(same_y, kinetic_weight(dx), 0.0) + jnp.where(same_x, kinetic_weight(dy), 0.0)
    point = jnp.where(dz == 0, 1.0, 0.0).astype(jnp.bfloat16)
    along_high, along_low = split(kinetic_weight(dz))
    none = jnp.zeros_like(point)
    right = jnp.concatenate(
        [jnp.concatenate([point, along_high], 1), jnp.concatenate([none, point], 1)], 0
    )
    fine = jnp.concatenate([none, along_low], 1)
    for j in range(proj_ref.shape[1]):
        values = proj_ref[0, j : j + 1, :]
        left = jnp.concatenate([near * values, here * values], 1)
        high, low = split(left)
        both = dot(high, right, NT) + dot(low, right, NT)
        plain = both[:, nz:]
        acted = both[:, :nz] + dot(high, fine, NT) + pot_ref[...] * plain
        flat = out_ref.reshape(rows * out_ref.shape[1], nz)
        nj = proj_ref.shape[1]
        flat[pl.ds(j, rows, stride=2 * nj), :] = acted
        flat[pl.ds(nj + j, rows, stride=2 * nj), :] = plain


def project_kernel(chunk, pq_ref, v_ref, out_ref, over_ref):
    @pl.when(pl.program_id(0) == 0)
    def _():
        out_ref[...] = jnp.zeros_like(out_ref)
        over_ref[...] = jnp.zeros_like(over_ref)

    bands, _, nz = v_ref.shape
    flat = v_ref.reshape(bands * chunk, nz)
    for r in range(0, chunk, 2):
        pq = jnp.concatenate([pq_ref[r], pq_ref[r + 1]], 1)
        v = jnp.concatenate(
            [flat[pl.ds(r, bands, stride=chunk), :], flat[pl.ds(r + 1, bands, stride=chunk), :]], 1
        )
        pq, v = split(pq), split(v)
        out_ref[...] += dot3(pq, v, NT)
        over_ref[...] += dot3(pq, pq, NT)


def local_kernel(parts, *refs):
    v_refs, (pot_ref, table_ref) = refs[:parts], refs[parts : parts + 2]
    out_refs, (pad_ref, mid_ref) = refs[parts + 2 : 2 * parts + 2], refs[2 * parts + 2 :]
    _, slab, ny, nz = v_refs[0].shape
    nx = parts * slab
    step = 4
    table_high, table_low = split(table_ref[...])
    both_rows = jnp.concatenate([table_high, table_high], 0)

    def fill(read):
        for p in range(parts):
            pad_ref[pl.ds(HALO + p * slab, slab)] = read(p)
        pad_ref[pl.ds(0, HALO)] = pad_ref[pl.ds(nx, HALO)]
        pad_ref[pl.ds(HALO + nx, HALO)] = pad_ref[pl.ds(HALO, HALO)]

    def apply(start):
        center = pad_ref[pl.ds(HALO + start, step)]
        total = (-center_weight) * center
        for k, weight in enumerate(stencil_weights, start=1):
            around = (
                pad_ref[pl.ds(HALO + start + k, step)]
                + pad_ref[pl.ds(HALO + start - k, step)]
                + pltpu.roll(center, k, 1)
                + pltpu.roll(center, ny - k, 1)
            )
            total = total + (-0.5 * weight) * around
        high, low = split(center.reshape(step * ny, nz))
        along = dot(jnp.concatenate([high, low], 1), both_rows, NN) + dot(high, table_low, NN)
        total = total + along.reshape(step, ny, nz)
        return total + (pot_ref[pl.ds(start, step)] - MIDDLE) * center

    fill(lambda p: v_refs[p][0])

    @pl.loop(0, nx // step)
    def _(i):
        mid_ref[pl.ds(i * step, step)] = SCALE_1 * apply(i * step)

    fill(lambda p: mid_ref[pl.ds(p * slab, slab)])

    for p in range(parts):

        @pl.loop(0, slab // step)
        def _(i, p=p):
            old = v_refs[p][0, pl.ds(i * step, step)]
            acted = apply(p * slab + i * step)
            out_refs[p][0, pl.ds(i * step, step)] = SCALE_2 * acted - SCALE_OLD * old


def expand_kernel(chunk, parts, halves, pos_ref, pq_ref, coef_ref, *refs):
    y_refs, (f_ref, g_ref) = refs[: parts * halves], refs[parts * halves :]
    each, _, nz = y_refs[0].shape
    bands = f_ref.shape[0]
    flat_y = [y_ref.reshape(each * chunk, nz) for y_ref in y_refs]
    flat_f = f_ref.reshape(bands * chunk, nz)
    coef = split(coef_ref[...])
    for r in range(chunk):
        added = dot3(coef, split(pq_ref[r]), NN)
        for p in range(parts):
            for h in range(halves):
                first = (p * halves + h) * each
                total = (
                    added[first : first + each]
                    + flat_y[p * halves + h][pl.ds(r, each, stride=chunk), :]
                )
                to = lax.rem(pos_ref[0] + p, parts) * (halves * each) + h * each
                flat_f[pl.ds(to * chunk + r, each, stride=chunk), :] = total
                g_ref[r, pl.ds(pl.multiple_of(to, each), each), :] = total


def gram_kernel(chunk, count, pos_ref, *refs):
    x_refs, (out_ref, x_scratch) = refs[:count], refs[count:]

    @pl.when(pl.program_id(0) == 0)
    def _():
        out_ref[...] = jnp.zeros_like(out_ref)

    _, bands, nz = x_refs[0].shape
    for r in range(0, chunk, 2):
        for p in range(count):
            at = pl.multiple_of(lax.rem(pos_ref[0] + count - p, count) * bands, bands)
            x_scratch[pl.ds(at, bands), :] = jnp.concatenate([x_refs[p][r], x_refs[p][r + 1]], 1)
        x = split(x_scratch[...])
        out_ref[...] += dot3(x, x, NT)


def shifted(values, axis, by):
    count = lax.axis_size(axis)
    return lax.ppermute(values, axis, [(i, (i + by) % count) for i in range(count)])


def summed_over(values, axis):
    count = lax.axis_size(axis)
    if count > 8:
        return lax.psum(values, axis)
    total = values
    for p in range(1, count):
        total = total + shifted(values, axis, p)
    return total


def block_of(values, index, count):
    size = values.shape[0] // count
    return lax.dynamic_slice_in_dim(values, index % count * size, size, 0)


def cost(flops, moved):
    return pl.CostEstimate(flops=flops, bytes_accessed=moved, transcendentals=0)


def call(kernel, **options):
    return pl.pallas_call(
        kernel, compiler_params=pltpu.CompilerParams(vmem_limit_bytes=VMEM), **options
    )


def per_device(orbitals, potential, projector, coupling, sphere_cells, atom_count):
    f32 = jnp.float32
    bands, slab, ny, nz = orbitals.shape
    slots, nj, sph = projector.shape
    nd, nb = lax.axis_size("domain"), lax.axis_size("band")
    nx, plane, rows = slab * nd, ny * nz, slab * ny
    pos = lax.axis_index("domain")
    share = bands // nd
    halves = 2 if share % 2 == 0 else 1
    each = share // halves

    packed = jnp.concatenate(
        [
            projector.reshape(slots * nj, sph),
            sphere_cells.astype(f32),
            jnp.pad(coupling, ((0, 0), (0, sph - nj))),
            potential.reshape(rows, nz),
        ],
        0,
    )
    packed = lax.all_gather(packed, "domain", axis=0, tiled=False)
    orbitals_later, packed = lax.optimization_barrier((orbitals, packed))
    ends = (slots * nj, slots * nj + slots, slots * nj + 2 * slots)
    proj_all = packed[:, : ends[0]].reshape(nd, slots, nj, sph)
    cells_all = packed[:, ends[0] : ends[1]].astype(jnp.int32)
    coupling_all = packed[:, ends[1] : ends[2], :nj].reshape(nd * slots, nj)
    pot_all = packed[:, ends[2] :].reshape(nx, ny, nz)

    pot_all = lax.dynamic_slice_in_dim(
        jnp.concatenate([pot_all, pot_all], 0), pos * slab, nx, 0
    )
    index = jnp.arange(nz, dtype=jnp.int32)
    table = kinetic_weight(periodic(index[:, None] - index[None, :], nz)).astype(f32)
    block = pl.BlockSpec((1, slab, ny, nz), lambda b: (b, 0, 0, 0))

    def sent(h, p):
        start = (pos - p) % nd * share + h * each
        part = lax.dynamic_slice_in_dim(orbitals_later, start, each, 0)
        return shifted(part, "domain", -p) if p else part

    local = []
    for h in range(halves):
        spread = [sent(h, p) for p in range(nd)]
        results = call(
            functools.partial(local_kernel, nd),
            grid=(each,),
            in_specs=[block] * nd
            + [
                pl.BlockSpec((nx, ny, nz), lambda b: (0, 0, 0)),
                pl.BlockSpec((nz, nz), lambda b: (0, 0)),
            ],
            out_specs=[block] * nd,
            out_shape=[jax.ShapeDtypeStruct(spread[0].shape, f32)] * nd,
            scratch_shapes=[
                pltpu.VMEM((nx + 2 * HALO, ny, nz), f32),
                pltpu.VMEM((nx, ny, nz), f32),
            ],
            cost_estimate=cost(share * nx * plane * 6000, share * nx * plane * 4),
        )(*spread, pot_all, table)
        local.append([shifted(part, "domain", p) if p else part for p, part in enumerate(results)])

    near = -(-(REACH + HALO) // slab)
    if nd <= 2 * near + 1:
        sources = jnp.arange(nd, dtype=jnp.int32)
    else:
        sources = (pos + jnp.arange(-near, near + 1, dtype=jnp.int32)) % nd
    atoms = sources.shape[0] * slots
    proj_near = proj_all[sources].reshape(atoms, nj, sph)
    cells = cells_all[sources].reshape(atoms, 1, sph)
    cell_x = (cells // plane - pos * slab) % nx
    per_atom = pl.BlockSpec((1, 1, sph), lambda a: (a, 0, 0))
    count = atoms * 2 * nj
    pq = call(
        functools.partial(build_kernel, nx, ny, slab),
        grid=(atoms,),
        in_specs=[
            per_atom,
            per_atom,
            per_atom,
            pl.BlockSpec((1, nj, sph), lambda a: (a, 0, 0)),
            pl.BlockSpec((rows, nz), lambda a: (0, 0)),
        ],
        out_specs=pl.BlockSpec((rows, 2 * nj, nz), lambda a: (0, a, 0)),
        out_shape=jax.ShapeDtypeStruct((rows, count, nz), f32),
        cost_estimate=cost(atoms * 600_000_000, rows * count * nz * 4),
    )(cell_x, cells // nz % ny, cells % nz, proj_near, potential.reshape(rows, nz))

    chunk = 8
    part_out, part_over = call(
        functools.partial(project_kernel, chunk),
        grid=(rows // chunk,),
        in_specs=[
            pl.BlockSpec((chunk, count, nz), lambda i: (i, 0, 0)),
            pl.BlockSpec((bands, chunk, nz), lambda i: (0, i, 0)),
        ],
        out_specs=[
            pl.BlockSpec((count, bands), lambda i: (0, 0)),
            pl.BlockSpec((count, count), lambda i: (0, 0)),
        ],
        out_shape=[
            jax.ShapeDtypeStruct((count, bands), f32),
            jax.ShapeDtypeStruct((count, count), f32),
        ],
        cost_estimate=cost(rows * nz * count * (count + bands) * 8, rows * count * nz * 4),
    )(pq, orbitals.reshape(bands, rows, nz))
    slot = jnp.arange(slots, dtype=jnp.int32)
    live = (slot[None, :] < atom_count[:, None]).reshape(-1)
    strength = jnp.where(live[:, None], coupling_all, 0.0)
    highest = lax.Precision.HIGHEST
    if count == nd * slots * 2 * nj:
        summed = lax.psum(jnp.concatenate([part_out, part_over], 1), "domain")
        both, over = summed[:, :bands], summed[:, bands:]
        strength = jnp.concatenate([jnp.zeros_like(strength), strength], 1).reshape(-1, 1)
        weight_0 = strength * both
        plain_1 = SCALE_1 * (
            jnp.roll(both, nj, 0) + jnp.dot(over, weight_0, precision=highest) - MIDDLE * both
        )
        coef = SCALE_2 * (
            strength * plain_1
            - (MIDDLE * SCALE_1) * weight_0
            + SCALE_1 * jnp.roll(weight_0, -nj, 0)
        )
    else:
        width, total = atoms * nj, nd * slots * nj
        out = part_out.reshape(atoms, 2, nj, bands)
        over = part_over.reshape(atoms, 2, nj, atoms, 2, nj)[:, 1, :, :, 1, :].reshape(width, width)
        both = jnp.concatenate([out[:, 0].reshape(width, bands), out[:, 1].reshape(width, bands)], 1)
        where = (sources[:, None] * (slots * nj) + jnp.arange(slots * nj)[None]).reshape(-1)
        both = jnp.zeros((total, 2 * bands), f32).at[where].set(both)
        over = jnp.zeros((total, total), f32).at[where[:, None], where[None, :]].set(over)
        both, over = lax.psum(both, "domain"), lax.psum(over, "domain")
        acted, plain = both[:, :bands], both[:, bands:]
        strength = strength.reshape(-1, 1)
        weight_0 = strength * plain
        plain_1 = SCALE_1 * (
            acted + jnp.dot(over, weight_0, precision=highest) - MIDDLE * plain
        )
        coef_p = SCALE_2 * (strength * plain_1 - (MIDDLE * SCALE_1) * weight_0)
        coef_q = (SCALE_2 * SCALE_1) * weight_0
        coef = jnp.stack(
            [coef_q.reshape(nd, slots, nj, bands), coef_p.reshape(nd, slots, nj, bands)], 2
        )
        coef = coef[sources].reshape(count, bands)
    coef = jnp.concatenate([coef, coef], 1).T
    coef = lax.dynamic_slice_in_dim(coef, pos * share, bands, 0)

    smem = pl.BlockSpec(memory_space=pltpu.SMEM)
    part_block = pl.BlockSpec((each, chunk, nz), lambda i: (0, i, 0))
    came = [local[h][(nd - p) % nd].reshape(each, rows, nz) for p in range(nd) for h in range(halves)]
    filtered, shared = call(
        functools.partial(expand_kernel, chunk, nd, halves),
        grid=(rows // chunk,),
        in_specs=[
            smem,
            pl.BlockSpec((chunk, count, nz), lambda i: (i, 0, 0)),
            pl.BlockSpec((bands, count), lambda i: (0, 0)),
        ]
        + [part_block] * (nd * halves),
        out_specs=[
            pl.BlockSpec((bands, chunk, nz), lambda i: (0, i, 0)),
            pl.BlockSpec((chunk, bands, nz), lambda i: (i, 0, 0)),
        ],
        out_shape=[
            jax.ShapeDtypeStruct((bands, rows, nz), f32),
            jax.ShapeDtypeStruct((rows, bands, nz), f32),
        ],
    )(pos.reshape(1), pq, coef, *came)

    band = lax.axis_index("band")
    given = [block_of(shared, band + p, nb) for p in range(nb)]
    given = [shifted(part, "band", p) if p else part for p, part in enumerate(given)]
    gram = call(
        functools.partial(gram_kernel, chunk, nb),
        grid=(rows // nb // chunk,),
        in_specs=[smem] + [pl.BlockSpec((chunk, bands, nz), lambda i: (i, 0, 0))] * nb,
        out_specs=pl.BlockSpec((nb * bands, nb * bands), lambda i: (0, 0)),
        out_shape=jax.ShapeDtypeStruct((nb * bands, nb * bands), f32),
        scratch_shapes=[pltpu.VMEM((nb * bands, 2 * nz), f32)],
    )(band.reshape(1), *given)
    own = block_of(gram, band, nb)
    for p in range(1, nb):
        own = own + shifted(block_of(gram, band + p, nb), "band", p)
    own = summed_over(own, "domain")
    return filtered.reshape(orbitals.shape), own / (nx * plane)


def solution(mesh):
    placed = (
        P("band", "domain", "groups", None),
        P("domain", "groups", None),
        P("domain", None, "groups"),
        P("domain", "groups"),
        P("domain", "groups"),
        P("groups"),
    )
    return jax.shard_map(
        per_device,
        mesh=mesh,
        in_specs=placed,
        out_specs=(P("band", "domain", "groups", None), P("band", "groups")),
        check_vma=False,
    )
```
